512 devices in a mesh: dp: 16 (over z_lo, x), expert: 32 (over z_hi, y, core).
Axes of the slice: x: 4, y: 4, z: 16 (z_hi: 4, z_lo: 4; z = z_hi * 4 + z_lo), core: 2. Of those that a mesh axis runs over, the one named last changes fastest.
Arguments:
- tokens: bfloat16 [2048, 4096], P(('dp', 'expert')), may hold values from -6 to 6
- expert_ids: int32 [2048, 2], P(('dp', 'expert')), may hold values from 0 to 31, all different within a row; in each aligned block of 128 rows (0 to 127, 128 to 255, ...) at most 16 rows name the same one
- route_weights: bfloat16 [2048, 2], P(('dp', 'expert')), may hold values from 0.099609375 to 1
- out_grad: bfloat16 [2048, 4096], P(('dp', 'expert')), may hold values from -6 to 6
- gate_weight: bfloat16 [32, 1536, 4096], P('expert', 'dp'), may hold values from -0.09375 to 0.09375
- up_weight: bfloat16 [32, 1536, 4096], P('expert', 'dp'), may hold values from -0.09375 to 0.09375
- down_weight: bfloat16 [32, 1536, 4096], P('expert', 'dp'), may hold values from -0.15625 to 0.15625
Outputs:
- mixed: bfloat16 [2048, 4096], P(('dp', 'expert'))
- input_grad: bfloat16 [2048, 4096], P(('dp', 'expert'))
- gate_grad: bfloat16 [32, 1536, 4096], P('expert', 'dp')
- up_grad: bfloat16 [32, 1536, 4096], P('expert', 'dp')
- down_grad: bfloat16 [32, 1536, 4096], P('expert', 'dp')
The draws below stay inside these ranges and needn't reach their ends.
Inputs may be any that keep to these rules, and one draw needn't show every extreme that they name: `expert_ids`: each row names 2 different experts. In each aligned block of 128 rows (the tokens of one index of dp) no expert is named by more than 16 rows, a bound that some block reaches.
All inputs are finite; a program needn't handle non-finite values.
Results may differ from the reference program's by a relative error of at most 0.024.
Values may be sent and summed in bfloat16 or wider, within the bound.
A program may use at most 64 MiB of HBM per device.

```python
import math
import jax
import jax.numpy as jnp
import numpy as np
from jax import lax

D = 4096
FF = 1536
TOP = 2
EXPERTS = 32
GROUP_TOK = 128
ROW_CAP = 16
TOKENS = 2048
N_DP = 16


def level_of(stream_key, extent, cuts, smallest, largest):
    level = 1.0
    for axis_at, parts in cuts:
        draws = jax.random.uniform(jax.random.fold_in(jax.random.fold_in(stream_key, 6), axis_at), (parts,), jnp.float32, smallest / len(cuts), largest / len(cuts))
        level = level * jnp.repeat(jnp.exp(draws), extent[axis_at] // parts).reshape((-1,) + (1,) * (len(extent) - 1 - axis_at))
    return level


def shared_out(stream_key, own, number, rows, amount, top, most, skew):
    sequence = jax.random.permutation(stream_key, amount)
    packed, ordinary = portions_of(amount, rows * top, most, skew, True), portions_of(amount, rows * top, most, skew, False)
    places = jnp.arange(amount)

    def named(tallies, turn):
        used = int((tallies > 0).sum())
        fixed = max(1, used // 4)
        moved = fixed + (places - fixed + turn * (used - fixed)) % max(1, amount - fixed)
        return jnp.zeros((amount,), jnp.int32).at[sequence[jnp.where(places < fixed, places, moved)]].set(jnp.asarray(tallies, jnp.int32))

    tallies = jnp.where(number % 4 == 0, named(packed, number // 4), named(ordinary, number - number // 4 - 1))
    mixed = jax.random.permutation(jax.random.fold_in(own, 3), amount)
    giver, sink = mixed[0:amount // 2 * 2:2], mixed[1:amount // 2 * 2:2]
    margin = jnp.minimum(tallies[giver] - 1, most - tallies[sink]) // 2
    margin = jnp.where((giver == sequence[0]) | (sink == sequence[0]) | (tallies[sink] == 0), 0, jnp.maximum(margin, 0))
    moved = jax.random.randint(jax.random.fold_in(own, 4), (amount // 2,), 0, 1 << 20) % (margin + 1)
    tallies = tallies.at[giver].add(-moved).at[sink].add(moved)
    labels = jnp.searchsorted(jnp.cumsum(tallies), jnp.arange(rows * top), side="right").astype(jnp.int32)
    listing = labels.reshape(top, rows).T
    listing = listing[jax.random.permutation(jax.random.fold_in(own, 1), rows)]
    turn = jax.random.randint(jax.random.fold_in(own, 2), (rows, 1), 0, top)
    return jnp.take_along_axis(listing, (jnp.arange(top)[None, :] + turn) % top, axis=1)


def portions_of(number_of, total, bound, skew, full):
    loads = [(1 << 20) // math.isqrt(standing ** skew) + 1 for standing in range(1, number_of + 1)]
    largest = bound if full else min(bound, max(-(-total // number_of), total * loads[0] // sum(loads)))
    least = 1 if total - largest >= number_of - 1 else 0
    given, rest = [largest] + [least] * (number_of - 1), total - largest - least * (number_of - 1)
    while rest > 0:
        free = [i for i in range(1, number_of) if given[i] < largest] or [i for i in range(1, number_of) if given[i] < bound]
        mass, remaining = sum([loads[i] for i in free]), rest
        for i in free:
            more = min(bound - given[i], max(1, remaining * loads[i] // mass), rest)
            given[i] = given[i] + more
            rest = rest - more
    return np.array(given)


def noise(key, shape, scale, reach, shards=(), held_as=jnp.bfloat16):
    values = jax.random.normal(key, shape, jnp.float32) * scale
    if len(shards) > 0:
        values = level_of(key, shape, shards, -0.22, 0.18) * values
    return jnp.clip(values, min=-reach, max=reach).astype(held_as)


def setup_inputs(seed: int = 0) -> dict:
    seeds = jax.random.split(jax.random.key(seed), 8)
    tokens = noise(seeds[0], (TOKENS, D), 1.0, 6.0, ((0, 512),))
    expert_ids_keys = jax.random.split(jax.random.fold_in(seeds[1], 1), TOKENS // GROUP_TOK)
    expert_ids_turns = jax.random.permutation(jax.random.fold_in(seeds[1], 3), TOKENS // GROUP_TOK)
    expert_ids = jax.vmap(lambda own, number: shared_out(jax.random.fold_in(seeds[1], 2), own, number, GROUP_TOK, EXPERTS, TOP, ROW_CAP, 2))(expert_ids_keys, expert_ids_turns).reshape((TOKENS, TOP))
    route_weights = jnp.clip(jnp.exp(math.log(1.0) - 2.306499 * jax.random.uniform(seeds[2], (TOKENS, TOP), jnp.float32) ** level_of(seeds[2], (TOKENS, TOP), ((0, 512),), -0.2, 0.2)), 0.099609375, 1.0).astype(jnp.bfloat16)
    out_grad = noise(seeds[3], (TOKENS, D), 1.0, 6.0, ((0, 512),))
    gate_weight = noise(seeds[4], (EXPERTS, FF, D), D ** -0.5, 0.09375, ((0, 32), (1, 16)))
    up_weight = noise(seeds[5], (EXPERTS, FF, D), D ** -0.5, 0.09375, ((0, 32), (1, 16)))
    down_weight = noise(seeds[6], (EXPERTS, FF, D), FF ** -0.5, 0.15625, ((0, 32), (1, 16)))
    return {"tokens": tokens, "expert_ids": expert_ids, "route_weights": route_weights, "out_grad": out_grad, "gate_weight": gate_weight, "up_weight": up_weight, "down_weight": down_weight}


def contract_rows(left, right):
    return lax.dot_general(left, right, (((1,), (1,)), ((), ())), preferred_element_type=jnp.float32)


def contract_first(left, right):
    return lax.dot_general(left, right, (((0,), (0,)), ((), ())), preferred_element_type=jnp.float32)


def grouped_sum(acts, weights):
    slot_total = acts.shape[0]
    group_width = FF // N_DP
    act_groups = acts.reshape(slot_total, N_DP, group_width).astype(jnp.float32)
    weight_groups = weights.reshape(N_DP, group_width, weights.shape[1]).astype(jnp.float32)
    partial_value = jnp.einsum("snf,nfd->nsd", act_groups, weight_groups)
    rounded = lax.optimization_barrier(partial_value.astype(jnp.bfloat16))
    return jnp.sum(rounded.astype(jnp.float32), axis=0)


def grouped_pair(first_acts, first_weights, second_acts, second_weights):
    slot_total = first_acts.shape[0]
    group_width = FF // N_DP
    width = first_weights.shape[1]
    first_groups = first_acts.reshape(slot_total, N_DP, group_width).astype(jnp.float32)
    second_groups = second_acts.reshape(slot_total, N_DP, group_width).astype(jnp.float32)
    partial_value = jnp.einsum("snf,nfd->nsd", first_groups, first_weights.reshape(N_DP, group_width, width).astype(jnp.float32))
    partial_value = partial_value + jnp.einsum("snf,nfd->nsd", second_groups, second_weights.reshape(N_DP, group_width, width).astype(jnp.float32))
    rounded = lax.optimization_barrier(partial_value.astype(jnp.bfloat16))
    return jnp.sum(rounded.astype(jnp.float32), axis=0)


def reference(tokens, expert_ids, route_weights, out_grad, gate_weight, up_weight, down_weight):
    token_count = tokens.shape[0]
    slot_total = N_DP * ROW_CAP
    positions = jnp.arange(token_count, dtype=jnp.int32)
    route_float = route_weights.astype(jnp.float32)
    grad_float = out_grad.astype(jnp.float32)

    def per_expert(totals, inputs):
        mixed_total, input_total = totals
        w_gate, w_up, w_down, expert = inputs
        matches = expert_ids == expert
        routed = jnp.any(matches, axis=1)
        weight = jnp.sum(jnp.where(matches, route_float, 0.0), axis=1)
        order_key = jnp.where(routed, positions, positions + token_count).astype(jnp.int32)
        slot_order = jnp.argsort(order_key)[:slot_total].astype(jnp.int32)
        slot_valid = routed[slot_order]
        slot_weight = jnp.where(slot_valid, weight[slot_order], 0.0)
        rows_x = jnp.where(slot_valid[:, None], tokens[slot_order], jnp.zeros((), jnp.bfloat16))
        rows_dy = (slot_weight[:, None] * grad_float[slot_order]).astype(jnp.bfloat16)
        gate_pre = contract_rows(rows_x, w_gate)
        up_pre = contract_rows(rows_x, w_up)
        gate_sig = jax.nn.sigmoid(gate_pre)
        silu_gate = gate_pre * gate_sig
        hidden = (silu_gate * up_pre).astype(jnp.bfloat16)
        expert_out = grouped_sum(hidden, w_down).astype(jnp.bfloat16)
        hidden_grad = contract_rows(rows_dy, w_down)
        silu_slope = gate_sig * (1.0 + gate_pre * (1.0 - gate_sig))
        gate_act = (hidden_grad * up_pre * silu_slope).astype(jnp.bfloat16)
        up_act = (hidden_grad * silu_gate).astype(jnp.bfloat16)
        grad_down = contract_first(hidden, rows_dy).astype(jnp.bfloat16)
        grad_gate = contract_first(gate_act, rows_x).astype(jnp.bfloat16)
        grad_up = contract_first(up_act, rows_x).astype(jnp.bfloat16)
        expert_in = grouped_pair(gate_act, w_gate, up_act, w_up).astype(jnp.bfloat16)
        mixed_total = mixed_total.at[slot_order].add(slot_weight[:, None] * expert_out.astype(jnp.float32))
        input_total = input_total.at[slot_order].add(jnp.where(slot_valid[:, None], expert_in.astype(jnp.float32), 0.0))
        return (mixed_total, input_total), (grad_gate, grad_up, grad_down)

    start_totals = (jnp.zeros(tokens.shape, jnp.float32), jnp.zeros(tokens.shape, jnp.float32))
    experts_all = jnp.arange(gate_weight.shape[0], dtype=jnp.int32)
    totals, grads = lax.scan(per_expert, start_totals, (gate_weight, up_weight, down_weight, experts_all))
    mixed = totals[0].astype(jnp.bfloat16)
    input_grad = totals[1].astype(jnp.bfloat16)
    return mixed, input_grad, grads[0], grads[1], grads[2]
```

```python
import functools

import jax
import jax.numpy as jnp
from jax import lax
from jax.experimental import pallas as pl
from jax.experimental.pallas import tpu as pltpu
from jax.sharding import PartitionSpec as P

SIZES = (4, 4, 4, 4, 2)
CHUNKS = 4
SLOTS = 16
META = 128
F32 = jnp.float32
BF16 = jnp.bfloat16
MESH = pl.DeviceIdType.MESH


def nt(left, right):
    return lax.dot_general(left, right, (((1,), (1,)), ((), ())), preferred_element_type=F32)


def iota(shape, dim):
    return lax.broadcasted_iota(jnp.int32, shape, dim)


def ones_where(mask):
    return jnp.where(mask, 1.0, 0.0).astype(F32)


class Comm:
    def __init__(self, send, recv):
        self.send, self.recv, self.count, self.sent = send, recv, 0, []

    def reserve(self, amount):
        at = self.count
        self.count += amount
        return at

    def start(self, src, dst, device, sem):
        copy = pltpu.make_async_remote_copy(
            src_ref=src, dst_ref=dst, send_sem=self.send.at[sem], recv_sem=self.recv.at[sem],
            device_id=device, device_id_type=MESH,
        )
        copy.start()
        self.sent.append(copy)

    def arrived(self, dst, device, sem):
        pltpu.make_async_remote_copy(
            src_ref=dst, dst_ref=dst, send_sem=self.send.at[sem], recv_sem=self.recv.at[sem],
            device_id=device, device_id_type=MESH,
        ).wait_recv()

    def drain(self):
        for copy in self.sent:
            copy.wait_send()


class RingGather:
    def __init__(self, comm, buf, index, size, device, turn):
        self.comm, self.buf, self.i, self.n, self.device = comm, buf, index, size, device
        self.d = 1 if turn % 2 == 0 else -1
        self.sem = comm.reserve(3) if size > 1 else 0

    def at(self, step):
        return lax.rem(self.i + step + self.n, self.n)

    def near(self):
        if self.n == 1:
            return
        for j, step in enumerate((self.d, -self.d)):
            self.comm.start(self.buf.at[self.i], self.buf.at[self.i], self.device(self.at(step)), self.sem + j)

    def far(self):
        if self.n == 1:
            return
        back, ahead = self.at(-self.d), self.at(self.d)
        self.comm.arrived(self.buf.at[back], self.device(back), self.sem)
        self.comm.start(self.buf.at[back], self.buf.at[back], self.device(ahead), self.sem + 2)

    def finish(self):
        if self.n == 1:
            return
        ahead = self.at(self.d)
        self.comm.arrived(self.buf.at[ahead], self.device(ahead), self.sem + 1)
        self.comm.arrived(self.buf.at[self.at(2)], self.device(self.at(-self.d)), self.sem + 2)


class RingReduce:
    def __init__(self, comm, buf, far_buf, near_buf, index, size, device, turn):
        self.comm, self.buf, self.far_buf, self.near_buf = comm, buf, far_buf, near_buf
        self.i, self.n, self.device = index, size, device
        self.d = 1 if turn % 2 == 0 else -1
        self.sem = comm.reserve(3) if size > 1 else 0

    def at(self, step):
        return lax.rem(self.i + step + self.n, self.n)

    def first(self):
        if self.n == 1:
            return
        ahead, back = self.at(self.d), self.at(-self.d)
        self.comm.start(self.buf.at[self.at(2)], self.far_buf, self.device(ahead), self.sem)
        self.comm.start(self.buf.at[back], self.near_buf.at[1], self.device(back), self.sem + 1)

    def second(self):
        if self.n == 1:
            return
        ahead, back = self.at(self.d), self.at(-self.d)
        self.comm.arrived(self.far_buf, self.device(back), self.sem)
        self.buf[ahead] = (self.buf[ahead].astype(F32) + self.far_buf[...].astype(F32)).astype(BF16)
        self.comm.start(self.buf.at[ahead], self.near_buf.at[0], self.device(ahead), self.sem + 2)

    def total(self):
        own = self.buf[self.i].astype(F32)
        if self.n == 1:
            return own
        ahead, back = self.at(self.d), self.at(-self.d)
        self.comm.arrived(self.near_buf.at[1], self.device(ahead), self.sem + 1)
        self.comm.arrived(self.near_buf.at[0], self.device(back), self.sem + 2)
        return own + self.near_buf[0].astype(F32) + self.near_buf[1].astype(F32)


def kernel(sizes, chunks, block, w_gate, w_up, w_down, out, g_gate, g_up, g_down, *scratch):
    n_zl, n_x, n_zh, n_y, n_c = sizes
    n_dp, n_ex = n_zl * n_x, n_zh * n_y * n_c
    lanes = n_ex * 8
    half = lanes // n_c
    ff, width = w_gate.shape[1], w_gate.shape[2]
    wc = width // chunks
    it = iter(scratch)
    per_chunk = lambda: [next(it) for _ in range(chunks)]
    got, slots, part, x_far, x_near, x_sum, z_near, pair, back, y_far, y_near, y_sum, h_far, h_near = (
        per_chunk() for _ in range(14)
    )
    wgu, wdn, ggu, gdn, picker, unpick, acc_gu, acc_d, act_t = (next(it) for _ in range(9))
    send, recv, local = (next(it) for _ in range(3))

    dp, ex = lax.axis_index("dp"), lax.axis_index("expert")
    x, zl = lax.rem(dp, n_x), lax.div(dp, n_x)
    c, y, zh = lax.rem(ex, n_c), lax.rem(lax.div(ex, n_c), n_y), lax.div(ex, n_c * n_y)

    to_x = lambda v: {"dp": zl * n_x + v, "expert": ex}
    to_zl = lambda v: {"dp": v * n_x + x, "expert": ex}
    to_c = lambda v: {"dp": dp, "expert": (zh * n_y + y) * n_c + v}
    to_y = lambda v: {"dp": dp, "expert": (zh * n_y + v) * n_c + c}
    to_zh = lambda v: {"dp": dp, "expert": (v * n_y + y) * n_c + c}

    loads = [
        pltpu.make_async_copy(w_gate.at[0], wgu.at[pl.ds(0, ff)], local.at[0]),
        pltpu.make_async_copy(w_up.at[0], wgu.at[pl.ds(ff, ff)], local.at[1]),
        pltpu.make_async_copy(w_down.at[0], wdn, local.at[2]),
    ]
    for load in loads:
        load.start()

    partners = []
    for index, size, to in ((x, n_x, to_x), (y, n_y, to_y), (zh, n_zh, to_zh)):
        if size > 1:
            partners += [to(lax.rem(index + 1, size)), to(lax.rem(index + size - 1, size))]
    partners += [to_zl(lax.rem(zl + j, n_zl)) for j in range(1, n_zl)]
    if n_c > 1:
        partners.append(to_c(1 - c))
    barrier = pltpu.get_barrier_semaphore()
    for partner in partners:
        pl.semaphore_signal(barrier, inc=1, device_id=partner, device_id_type=MESH)

    for k in range(chunks):
        lo = 0 if k == 0 else META + k * wc
        got[k][c, y, zh] = block[:, lo : META + (k + 1) * wc]
    pl.semaphore_wait(barrier, len(partners))

    comm = Comm(send, recv)
    in_zh = [RingGather(comm, got[k].at[c, y], zh, n_zh, to_zh, k) for k in range(chunks)]
    in_y = [RingGather(comm, got[k].at[c], y, n_y, to_y, k) for k in range(chunks)]
    in_c = [comm.reserve(1) for k in range(chunks)]
    in_zl = [comm.reserve(3) for k in range(chunks)]
    in_x = [RingGather(comm, slots[k], x, n_x, to_x, k) for k in range(chunks)]
    out_x = [RingReduce(comm, part[k], x_far[k], x_near[k], x, n_x, to_x, k) for k in range(chunks)]
    out_zl = [comm.reserve(3) for k in range(chunks)]
    out_c = [comm.reserve(1) for k in range(chunks)]
    out_y = [RingReduce(comm, back[k], y_far[k], y_near[k], y, n_y, to_y, k) for k in range(chunks)]
    out_zh = [RingReduce(comm, y_sum[k], h_far[k], h_near[k], zh, n_zh, to_zh, k) for k in range(chunks)]

    def make_pickers():
        meta = got[0][:, :, :, :, :META].astype(F32).reshape(lanes, META).astype(BF16)
        eye = ones_where(iota((8, META), 0) == iota((8, META), 1)).astype(BF16)
        facts = nt(eye, meta)
        id0, id1, w0, w1 = (facts[j : j + 1] for j in range(4))
        same = (iota((lanes, lanes), 0) % 8 < 4) == (iota((lanes, lanes), 1) % 8 < 4)
        before = ones_where((iota((lanes, lanes), 0) < iota((lanes, lanes), 1)) & same).astype(BF16)
        slot = iota((2 * SLOTS, lanes), 0)
        is_x = slot < SLOTS
        fits = ones_where(is_x == (iota((2 * SLOTS, lanes), 1) % 8 < 4))
        slot_f = (slot % SLOTS).astype(F32)
        returns = []
        for j in range(n_c):
            expert = (ex if j == 0 else ex + 1 - 2 * c).astype(F32)
            m0, m1 = ones_where(id0 == expert), ones_where(id1 == expert)
            routed = m0 + m1
            weight = m0 * w0 + m1 * w1
            rank = jnp.dot(
                jnp.broadcast_to(routed, (8, lanes)).astype(BF16), before, preferred_element_type=F32
            )[0:1]
            hit = fits * ones_where(slot_f == rank) * routed
            if j == 0:
                picker[...] = jnp.where(is_x, hit, hit * weight).astype(BF16)
            returns.append(jnp.where(is_x, hit * weight, hit))
        flat = jnp.transpose(returns[0] if n_c == 1 else jnp.concatenate(returns, axis=0))
        if n_c == 1:
            unpick[...] = flat.astype(BF16)
        else:
            unpick[...] = jnp.where(c == 0, flat[:half], flat[half:]).astype(BF16)


    def in_core(k):
        in_y[k].finish()
        if n_c > 1:
            comm.start(got[k].at[c], got[k].at[c], to_c(1 - c), in_c[k])

    def in_pick(k):
        if n_c > 1:
            comm.arrived(got[k].at[1 - c], to_c(1 - c), in_c[k])
        if k == 0:
            make_pickers()
        lo = META if k == 0 else 0
        rows = got[k][:, :, :, :, lo:].astype(F32).reshape(lanes, wc).astype(BF16)
        slots[k][x, zl] = jnp.dot(picker[...], rows, preferred_element_type=F32).astype(BF16)
        for j in range(1, n_zl):
            comm.start(slots[k].at[x, zl], slots[k].at[x, zl], to_zl(lax.rem(zl + j, n_zl)), in_zl[k] + j - 1)

    def in_lines(k):
        for j in range(1, n_zl):
            source = lax.rem(zl + n_zl - j, n_zl)
            comm.arrived(slots[k].at[x, source], to_zl(source), in_zl[k] + j - 1)
        in_x[k].near()

    def rows_of(k, at):
        return slots[k][:, :, at : at + SLOTS].reshape(n_dp * SLOTS, wc)

    def in_products(k):
        in_x[k].finish()
        if k == 0:
            for load in loads:
                load.wait()
        cols = slice(k * wc, (k + 1) * wc)
        gu = nt(wgu[:, cols], rows_of(k, 0))
        dn = nt(wdn[:, cols], rows_of(k, SLOTS))
        acc_gu[...] = gu if k == 0 else acc_gu[...] + gu
        acc_d[...] = dn if k == 0 else acc_d[...] + dn

    def in_y_near(k):
        in_zh[k].finish()
        in_y[k].near()

    stages = [
        lambda k: in_zh[k].near(),
        lambda k: in_zh[k].far(),
        in_y_near,
        lambda k: in_y[k].far(),
        in_core,
        in_pick,
        in_lines,
        lambda k: in_x[k].far(),
        in_products,
    ]
    for tick in range(chunks + len(stages) - 1):
        for s in reversed(range(len(stages))):
            if 0 <= tick - s < chunks:
                stages[s](tick - s)


    gate, up, hid_grad = acc_gu[:ff], acc_gu[ff:], acc_d[...]
    sig = jax.nn.sigmoid(gate)
    silu = gate * sig
    hidden = silu * up
    gate_act = hid_grad * up * (sig * (1.0 + gate * (1.0 - sig)))
    up_act = hid_grad * silu
    stacked = jnp.concatenate([hidden, gate_act, up_act], axis=0)
    act_t[0:ff] = hidden.astype(BF16)
    act_t[ff : 2 * ff] = gate_act.astype(BF16)
    act_t[2 * ff : 3 * ff] = up_act.astype(BF16)
    turned = jnp.transpose(stacked).astype(BF16)


    def out_products(k):
        cols = slice(k * wc, (k + 1) * wc)
        shape = (n_x, n_zl, SLOTS, wc)
        o = jnp.dot(turned[:, :ff], wdn[:, cols], preferred_element_type=F32)
        part[k][:, :, 0:SLOTS] = o.astype(BF16).reshape(shape)
        i = jnp.dot(turned[:, ff:], wgu[:, cols], preferred_element_type=F32)
        part[k][:, :, SLOTS:] = i.astype(BF16).reshape(shape)
        out_x[k].first()

    def out_second(k):
        out_x[k].second()
        cols = slice(k * wc, (k + 1) * wc)
        gdn[:, cols] = jnp.dot(act_t[0:ff], rows_of(k, SLOTS), preferred_element_type=F32).astype(BF16)
        ggu[:, cols] = jnp.dot(act_t[ff:], rows_of(k, 0), preferred_element_type=F32).astype(BF16)

    def out_lines(k):
        x_sum[k][...] = out_x[k].total().astype(BF16)
        for j in range(1, n_zl):
            target = lax.rem(zl + j, n_zl)
            comm.start(x_sum[k].at[target], z_near[k].at[j - 1], to_zl(target), out_zl[k] + j - 1)

    def out_core(k):
        total = x_sum[k][zl].astype(F32)
        for j in range(1, n_zl):
            comm.arrived(z_near[k].at[j - 1], to_zl(lax.rem(zl + n_zl - j, n_zl)), out_zl[k] + j - 1)
            total = total + z_near[k][j - 1].astype(F32)
        pair[k][0] = total.astype(BF16)
        if n_c > 1:
            comm.start(pair[k].at[0], pair[k].at[1], to_c(1 - c), out_c[k])

    def out_unpick(k):
        if n_c > 1:
            comm.arrived(pair[k].at[1], to_c(1 - c), out_c[k])
        rows = pair[k][...].reshape(n_c * 2 * SLOTS, wc)
        spread = jnp.dot(unpick[...], rows, preferred_element_type=F32)
        back[k][...] = spread.reshape(n_y, n_zh, 8, wc).astype(BF16)
        out_y[k].first()

    def out_zh_first(k):
        y_sum[k][...] = out_y[k].total().astype(BF16)
        out_zh[k].first()

    def out_store(k):
        out[:, k * wc : (k + 1) * wc] = out_zh[k].total().astype(BF16)

    stages = [
        out_products,
        out_second,
        out_lines,
        out_core,
        out_unpick,
        lambda k: out_y[k].second(),
        out_zh_first,
        lambda k: out_zh[k].second(),
        out_store,
    ]
    stores = []
    for tick in range(chunks + len(stages) - 1):
        for s in reversed(range(len(stages))):
            if 0 <= tick - s < chunks:
                stages[s](tick - s)
        if tick == chunks:
            stores += [
                pltpu.make_async_copy(ggu.at[pl.ds(0, ff)], g_gate.at[0], local.at[3]),
                pltpu.make_async_copy(ggu.at[pl.ds(ff, ff)], g_up.at[0], local.at[4]),
                pltpu.make_async_copy(gdn, g_down.at[0], local.at[5]),
            ]
            for store in stores:
                store.start()
    comm.drain()
    for store in stores:
        store.wait()


def shards(sizes, chunks, tokens, expert_ids, route_weights, out_grad, gate_weight, up_weight, down_weight):
    n_zl, n_x, n_zh, n_y, n_c = sizes
    n_dp, n_ex = n_zl * n_x, n_zh * n_y * n_c
    _, ff, width = gate_weight.shape
    wc = width // chunks
    lanes = n_ex * 8
    facts = jnp.concatenate([expert_ids.astype(BF16), route_weights], axis=1)
    facts = jnp.pad(facts, ((0, 0), (0, META - 4)))
    block = jnp.concatenate(
        [jnp.concatenate([facts, tokens], axis=1), jnp.concatenate([facts, out_grad], axis=1)], axis=0
    )
    vm = lambda *shape: pltpu.VMEM(shape, BF16)
    each = lambda *shape: [vm(*shape) for _ in range(chunks)]
    copies = chunks * 26
    scratch = (
        [vm(n_c, n_y, n_zh, 8, wc + (META if k == 0 else 0)) for k in range(chunks)]
        + each(n_x, n_zl, 2 * SLOTS, wc)
        + each(n_x, n_zl, 2 * SLOTS, wc)
        + each(n_zl, 2 * SLOTS, wc)
        + each(2, n_zl, 2 * SLOTS, wc)
        + each(n_zl, 2 * SLOTS, wc)
        + each(3, 2 * SLOTS, wc)
        + each(n_c, 2 * SLOTS, wc)
        + each(n_y, n_zh, 8, wc)
        + each(n_zh, 8, wc)
        + each(2, n_zh, 8, wc)
        + each(n_zh, 8, wc)
        + each(8, wc)
        + each(2, 8, wc)
        + [
            vm(2 * ff, width), vm(ff, width), vm(2 * ff, width), vm(ff, width),
            vm(2 * SLOTS, lanes), vm(lanes // n_c, n_c * 2 * SLOTS),
            pltpu.VMEM((2 * ff, n_dp * SLOTS), F32), pltpu.VMEM((ff, n_dp * SLOTS), F32),
            vm(3 * ff, n_dp * SLOTS),
            pltpu.SemaphoreType.DMA((copies,)), pltpu.SemaphoreType.DMA((copies,)),
            pltpu.SemaphoreType.DMA((6,)),
        ]
    )
    any_space = pl.BlockSpec(memory_space=pl.ANY)
    vmem = pl.BlockSpec(memory_space=pltpu.VMEM)
    rows, g_gate, g_up, g_down = pl.pallas_call(
        functools.partial(kernel, sizes, chunks),
        out_shape=(
            jax.ShapeDtypeStruct((8, width), BF16),
            jax.ShapeDtypeStruct(gate_weight.shape, BF16),
            jax.ShapeDtypeStruct(gate_weight.shape, BF16),
            jax.ShapeDtypeStruct(gate_weight.shape, BF16),
        ),
        in_specs=[vmem, any_space, any_space, any_space],
        out_specs=(vmem, any_space, any_space, any_space),
        scratch_shapes=scratch,
        compiler_params=pltpu.CompilerParams(
            collective_id=0, has_side_effects=True, vmem_limit_bytes=56 * 2**20
        ),
        name="experts",
    )(block, gate_weight, up_weight, down_weight)
    return rows[:4], rows[4:], g_gate, g_up, g_down


def solution(mesh):
    rows, held = P(("dp", "expert"), None), P("expert", "dp", None)
    return jax.shard_map(
        functools.partial(shards, SIZES, CHUNKS),
        mesh=mesh,
        in_specs=(rows, rows, rows, rows, held, held, held),
        out_specs=(rows, rows, held, held, held),
        check_vma=False,
    )
```

```python
import functools

import jax
import jax.numpy as jnp
from jax import lax
from jax.experimental import pallas as pl
from jax.experimental.pallas import tpu as pltpu
from jax.sharding import PartitionSpec as P

SIZES = (4, 4, 4, 4, 2)
PIECES = 4
ORDER = (
    0, 1, 2, 10, 3, 11, 4, 12, 5, 20, 13, 6, 21, 14, 7, 22, 15, 30, 23, 16, 24, 40, 31, 17, 25, 41, 32, 26, 42, 33, 43,
    34, 50, 27, 44, 35, 51, 45, 36, 60, 46, 52, 37, 61, 47, 53, 70, 54, 62, 71, 55, 63, 56, 64, 57, 72, 65, 73, 81, 90,
    91, 66, 74, 67, 75, 100, 92, 101, 93, 76, 77, 82, 110, 120, 111, 112, 121, 102, 94, 113, 130, 103, 95, 140, 122, 131,
    114, 115, 141, 104, 96, 123, 150, 116, 132, 117, 151, 142, 105, 124, 97, 133, 160, 143, 161, 152, 106, 125, 134, 170,
    107, 144, 162, 153, 171, 126, 135, 127, 163, 145, 154, 172, 136, 146, 155, 137, 173, 164, 147, 165, 156, 174, 157,
    175, 166, 167, 176, 177,
)
SLOTS = 16
META = 128
F32 = jnp.float32
BF16 = jnp.bfloat16
MESH = pl.DeviceIdType.MESH


def nt(left, right):
    return lax.dot_general(left, right, (((1,), (1,)), ((), ())), preferred_element_type=F32)


def iota(shape, dim):
    return lax.broadcasted_iota(jnp.int32, shape, dim)


def ones_where(mask):
    return jnp.where(mask, 1.0, 0.0).astype(F32)


class Comm:
    def __init__(self, send, recv):
        self.send, self.recv, self.count, self.sent = send, recv, 0, []

    def reserve(self, amount):
        at = self.count
        self.count += amount
        return at

    def start(self, src, dst, device, sem):
        copy = pltpu.make_async_remote_copy(
            src_ref=src, dst_ref=dst, send_sem=self.send.at[sem], recv_sem=self.recv.at[sem],
            device_id=device, device_id_type=MESH,
        )
        copy.start()
        self.sent.append(copy)

    def arrived(self, dst, device, sem):
        pltpu.make_async_remote_copy(
            src_ref=dst, dst_ref=dst, send_sem=self.send.at[sem], recv_sem=self.recv.at[sem],
            device_id=device, device_id_type=MESH,
        ).wait_recv()

    def drain(self):
        for copy in self.sent:
            copy.wait_send()


class RingGather:
    def __init__(self, comm, buf, index, size, device, turn):
        self.comm, self.buf, self.i, self.n, self.device = comm, buf, index, size, device
        self.d = 1 if turn % 2 == 0 else -1
        self.sem = comm.reserve(3) if size > 1 else 0

    def at(self, step):
        return lax.rem(self.i + step + self.n, self.n)

    def near(self):
        if self.n == 1:
            return
        for j, step in enumerate((self.d, -self.d)):
            self.comm.start(self.buf.at[self.i], self.buf.at[self.i], self.device(self.at(step)), self.sem + j)

    def far(self):
        if self.n == 1:
            return
        back, ahead = self.at(-self.d), self.at(self.d)
        self.comm.arrived(self.buf.at[back], self.device(back), self.sem)
        self.comm.start(self.buf.at[back], self.buf.at[back], self.device(ahead), self.sem + 2)

    def finish(self):
        if self.n == 1:
            return
        ahead = self.at(self.d)
        self.comm.arrived(self.buf.at[ahead], self.device(ahead), self.sem + 1)
        self.comm.arrived(self.buf.at[self.at(2)], self.device(self.at(-self.d)), self.sem + 2)


class Spread:
    def __init__(self, comm, buf, index, size, device):
        self.comm, self.buf, self.i, self.n, self.device = comm, buf, index, size, device
        self.sem = comm.reserve(size - 1)

    def send(self):
        for j in range(1, self.n):
            self.comm.start(
                self.buf.at[self.i], self.buf.at[self.i], self.device(lax.rem(self.i + j, self.n)), self.sem + j - 1
            )

    def finish(self):
        for j in range(1, self.n):
            source = lax.rem(self.i + self.n - j, self.n)
            self.comm.arrived(self.buf.at[source], self.device(source), self.sem + j - 1)


class Collect:
    def __init__(self, comm, buf, near_buf, index, size, device):
        self.comm, self.buf, self.near_buf, self.i, self.n, self.device = comm, buf, near_buf, index, size, device
        self.sem = comm.reserve(size - 1)

    def send(self):
        for j in range(1, self.n):
            target = lax.rem(self.i + j, self.n)
            self.comm.start(self.buf.at[target], self.near_buf.at[j - 1], self.device(target), self.sem + j - 1)

    def total(self):
        value = self.buf[self.i].astype(F32)
        for j in range(1, self.n):
            source = lax.rem(self.i + self.n - j, self.n)
            self.comm.arrived(self.near_buf.at[j - 1], self.device(source), self.sem + j - 1)
            value = value + self.near_buf[j - 1].astype(F32)
        return value


class RingReduce:
    def __init__(self, comm, buf, far_buf, near_buf, index, size, device, turn):
        self.comm, self.buf, self.far_buf, self.near_buf = comm, buf, far_buf, near_buf
        self.i, self.n, self.device = index, size, device
        self.d = 1 if turn % 2 == 0 else -1
        self.sem = comm.reserve(3) if size > 1 else 0

    def at(self, step):
        return lax.rem(self.i + step + self.n, self.n)

    def first(self):
        if self.n == 1:
            return
        ahead, back = self.at(self.d), self.at(-self.d)
        self.comm.start(self.buf.at[self.at(2)], self.far_buf, self.device(ahead), self.sem)
        self.comm.start(self.buf.at[back], self.near_buf.at[1], self.device(back), self.sem + 1)

    def second(self):
        if self.n == 1:
            return
        ahead, back = self.at(self.d), self.at(-self.d)
        self.comm.arrived(self.far_buf, self.device(back), self.sem)
        self.buf[ahead] = (self.buf[ahead].astype(F32) + self.far_buf[...].astype(F32)).astype(BF16)
        self.comm.start(self.buf.at[ahead], self.near_buf.at[0], self.device(ahead), self.sem + 2)

    def total(self):
        own = self.buf[self.i].astype(F32)
        if self.n == 1:
            return own
        ahead, back = self.at(self.d), self.at(-self.d)
        self.comm.arrived(self.near_buf.at[1], self.device(ahead), self.sem + 1)
        self.comm.arrived(self.near_buf.at[0], self.device(back), self.sem + 2)
        return own + self.near_buf[0].astype(F32) + self.near_buf[1].astype(F32)


def kernel(
    sizes, pieces, tokens, out_grad, meta, w_gate, w_up, w_down, mixed, in_grad, g_gate, g_up, g_down, *scratch
):
    n_zl, n_x, n_zh, n_y, n_c = sizes
    n_dp, n_ex = n_zl * n_x, n_zh * n_y * n_c
    lanes = n_ex * 8
    half = lanes // n_c
    ff, width = w_gate.shape[1], w_gate.shape[2]
    wc = width // pieces
    hw = wc // 2
    items = range(2 * pieces)
    it = iter(scratch)
    per_item = lambda: [next(it) for _ in items]
    got, slots, part, x_far, x_near, x_sum, z_near, pair, back, y_near, y_sum, h_far, h_near = (
        per_item() for _ in range(13)
    )
    wgu, wdn, ggu, gdn, pick_x, pick_g, back_o, back_i, acc_gu, acc_d, hid, hid_t, gu, gu_t = (
        next(it) for _ in range(14)
    )
    send, recv, local = (next(it) for _ in range(3))

    dp, ex = lax.axis_index("dp"), lax.axis_index("expert")
    x, zl = lax.rem(dp, n_x), lax.div(dp, n_x)
    c, y, zh = lax.rem(ex, n_c), lax.rem(lax.div(ex, n_c), n_y), lax.div(ex, n_c * n_y)

    to_x = lambda v: {"dp": zl * n_x + v, "expert": ex}
    to_zl = lambda v: {"dp": v * n_x + x, "expert": ex}
    to_c = lambda v: {"dp": dp, "expert": (zh * n_y + y) * n_c + v}
    to_y = lambda v: {"dp": dp, "expert": (zh * n_y + v) * n_c + c}
    to_zh = lambda v: {"dp": dp, "expert": (v * n_y + y) * n_c + c}

    partners = []
    for index, size, to in ((x, n_x, to_x), (zh, n_zh, to_zh)):
        if size > 1:
            partners += [to(lax.rem(index + 1, size)), to(lax.rem(index + size - 1, size))]
    partners += [to_zl(lax.rem(zl + j, n_zl)) for j in range(1, n_zl)]
    partners += [to_y(lax.rem(y + j, n_y)) for j in range(1, n_y)]
    if n_c > 1:
        partners.append(to_c(1 - c))
    barrier = pltpu.get_barrier_semaphore()
    for partner in partners:
        pl.semaphore_signal(barrier, inc=1, device_id=partner, device_id_type=MESH)

    loads = [
        pltpu.make_async_copy(w_gate.at[0], wgu.at[pl.ds(0, ff)], local.at[0]),
        pltpu.make_async_copy(w_up.at[0], wgu.at[pl.ds(ff, ff)], local.at[1]),
        pltpu.make_async_copy(w_down.at[0], wdn, local.at[2]),
    ]
    for load in loads:
        load.start()

    def piece(k):
        lo = k % pieces * wc
        return slice(lo, lo + wc)

    for k in items:
        source, lo = tokens if k < pieces else out_grad, k % pieces * wc
        own = jnp.concatenate(
            [source[:, lo : lo + hw].astype(F32), source[:, lo + hw : lo + wc].astype(F32)], axis=0
        ).astype(BF16)
        if k == 0:
            got[k][c, y, zh, :, :META] = meta[...]
            got[k][c, y, zh, :, META:] = own
        else:
            got[k][c, y, zh] = own
    pl.semaphore_wait(barrier, len(partners))

    comm = Comm(send, recv)
    in_zh = [RingGather(comm, got[k].at[c, y], zh, n_zh, to_zh, k) for k in items]
    in_y = [Spread(comm, got[k].at[c], y, n_y, to_y) for k in items]
    in_c = [comm.reserve(1) for k in items]
    in_zl = [Spread(comm, slots[k].at[x], zl, n_zl, to_zl) for k in items]
    in_x = [RingGather(comm, slots[k], x, n_x, to_x, k) for k in items]
    out_x = [RingReduce(comm, part[k], x_far[k], x_near[k], x, n_x, to_x, k) for k in items]
    out_zl = [Collect(comm, x_sum[k], z_near[k], zl, n_zl, to_zl) for k in items]
    out_c = [comm.reserve(1) for k in items]
    out_y = [Collect(comm, back[k], y_near[k], y, n_y, to_y) for k in items]
    out_zh = [RingReduce(comm, y_sum[k], h_far[k], h_near[k], zh, n_zh, to_zh, k) for k in items]

    def make_pickers():
        rows = got[0][:, :, :, :, :META].astype(F32).reshape(lanes, META).astype(BF16)
        eye = ones_where(iota((8, META), 0) == iota((8, META), 1)).astype(BF16)
        facts = nt(eye, rows)
        id0, id1, w0, w1 = (facts[j : j + 1] for j in range(4))
        same = (iota((lanes, lanes), 0) % 8 < 4) == (iota((lanes, lanes), 1) % 8 < 4)
        before = ones_where((iota((lanes, lanes), 0) < iota((lanes, lanes), 1)) & same).astype(BF16)
        slot = iota((2 * SLOTS, lanes), 0)
        fits = ones_where((slot < SLOTS) == (iota((2 * SLOTS, lanes), 1) % 8 < 4))
        slot_f = (slot % SLOTS).astype(F32)
        plain, weighted = [], []
        for j in range(n_c):
            expert = (ex if j == 0 else ex + 1 - 2 * c).astype(F32)
            m0, m1 = ones_where(id0 == expert), ones_where(id1 == expert)
            routed = m0 + m1
            rank = jnp.dot(
                jnp.broadcast_to(routed, (8, lanes)).astype(BF16), before, preferred_element_type=F32
            )[0:1]
            hit = fits * ones_where(slot_f == rank) * routed
            plain.append(hit)
            weighted.append(hit * (m0 * w0 + m1 * w1))
        pick_x[...] = plain[0].astype(BF16)
        pick_g[...] = weighted[0].astype(BF16)
        for ref, parts in ((back_i, plain), (back_o, weighted)):
            flat = jnp.transpose(parts[0] if n_c == 1 else jnp.concatenate(parts, axis=0))
            ref[...] = (flat if n_c == 1 else jnp.where(c == 0, flat[:half], flat[half:])).astype(BF16)


    def in_y_send(k):
        in_zh[k].finish()
        in_y[k].send()

    def in_core(k):
        in_y[k].finish()
        if n_c > 1:
            comm.start(got[k].at[c], got[k].at[c], to_c(1 - c), in_c[k])

    def in_pick(k):
        if n_c > 1:
            comm.arrived(got[k].at[1 - c], to_c(1 - c), in_c[k])
        if k == 0:
            make_pickers()
        lo = META if k == 0 else 0
        rows = got[k][:, :, :, :, lo:].astype(F32).reshape(lanes, hw).astype(BF16)
        picker = pick_x if k < pieces else pick_g
        picked = jnp.dot(picker[...], rows, preferred_element_type=F32).astype(BF16)
        slots[k][x, zl, :, :hw] = picked[:SLOTS]
        slots[k][x, zl, :, hw:] = picked[SLOTS:]
        in_zl[k].send()

    def in_x_near(k):
        in_zl[k].finish()
        in_x[k].near()

    def rows_of(k):
        return slots[k][...].reshape(n_dp * SLOTS, wc)

    def in_products(k):
        in_x[k].finish()
        if k == 0:
            for load in loads:
                load.wait()
        weights, total = (wgu, acc_gu) if k < pieces else (wdn, acc_d)
        product = nt(weights[:, piece(k)], rows_of(k))
        total[...] = product if k % pieces == 0 else total[...] + product


    def activate(k):
        if k == 1:
            gate, up = acc_gu[:ff], acc_gu[ff:]
            sig = jax.nn.sigmoid(gate)
            silu = gate * sig
            hidden = silu * up
            hid[...] = hidden.astype(BF16)
            hid_t[...] = jnp.transpose(hidden).astype(BF16)
            acc_gu[:ff] = up * (sig * (1.0 + gate * (1.0 - sig)))
            acc_gu[ff:] = silu
        else:
            grad = acc_d[...]
            both = jnp.concatenate([grad * acc_gu[:ff], grad * acc_gu[ff:]], axis=0)
            gu[...] = both.astype(BF16)
            gu_t[...] = jnp.transpose(both).astype(BF16)


    def out_products(k):
        left, weights = (hid_t, wdn) if k < pieces else (gu_t, wgu)
        product = jnp.dot(left[...], weights[:, piece(k)], preferred_element_type=F32)
        part[k][...] = product.astype(BF16).reshape(n_x, n_zl, SLOTS, wc)
        out_x[k].first()

    stores = []

    def weight_grads(k):
        left, held = (gu, ggu) if k < pieces else (hid, gdn)
        held[:, piece(k)] = jnp.dot(left[...], rows_of(k), preferred_element_type=F32).astype(BF16)
        pairs = ((ggu, 0, g_gate), (ggu, ff, g_up)) if k < pieces else ((gdn, 0, g_down),)
        for ref, at, target in pairs:
            store = pltpu.make_async_copy(
                ref.at[pl.ds(at, ff), piece(k)], target.at[0, :, piece(k)], local.at[3 + len(stores)]
            )
            store.start()
            stores.append(store)

    def out_lines(k):
        x_sum[k][...] = out_x[k].total().astype(BF16)
        out_zl[k].send()

    def out_core(k):
        total = out_zl[k].total().astype(BF16)
        pair[k][0, :SLOTS] = total[:, :hw]
        pair[k][0, SLOTS:] = total[:, hw:]
        if n_c > 1:
            comm.start(pair[k].at[0], pair[k].at[1], to_c(1 - c), out_c[k])

    def out_back(k):
        if n_c > 1:
            comm.arrived(pair[k].at[1], to_c(1 - c), out_c[k])
        rows = pair[k][...].reshape(n_c * 2 * SLOTS, hw)
        spread = jnp.dot((back_o if k < pieces else back_i)[...], rows, preferred_element_type=F32)
        back[k][...] = spread.reshape(n_y, n_zh, 8, hw).astype(BF16)
        out_y[k].send()

    def out_zh_first(k):
        y_sum[k][...] = out_y[k].total().astype(BF16)
        out_zh[k].first()

    def out_store(k):
        total = out_zh[k].total()
        target, lo = mixed if k < pieces else in_grad, k % pieces * wc
        target[:, lo : lo + hw] = total[:4].astype(BF16)
        target[:, lo + hw : lo + wc] = total[4:].astype(BF16)

    steps = (
        lambda k: in_zh[k].near(),
        lambda k: in_zh[k].far(),
        in_y_send,
        in_core,
        in_pick,
        in_x_near,
        lambda k: in_x[k].far(),
        in_products,
        activate,
        out_products,
        lambda k: out_x[k].second(),
        weight_grads,
        out_lines,
        out_core,
        out_back,
        out_zh_first,
        lambda k: out_zh[k].second(),
        out_store,
    )
    for entry in ORDER:
        steps[entry // 10](entry % 10)
    comm.drain()
    for store in stores:
        store.wait()


def shards(sizes, pieces, tokens, expert_ids, route_weights, out_grad, gate_weight, up_weight, down_weight):
    n_zl, n_x, n_zh, n_y, n_c = sizes
    n_dp, n_ex = n_zl * n_x, n_zh * n_y * n_c
    _, ff, width = gate_weight.shape
    wc = width // pieces
    hw = wc // 2
    lanes = n_ex * 8
    facts = jnp.concatenate([expert_ids.astype(BF16), route_weights], axis=1)
    meta = jnp.pad(jnp.concatenate([facts, facts], axis=0), ((0, 0), (0, META - 4)))
    vm = lambda *shape: pltpu.VMEM(shape, BF16)
    fl = lambda *shape: pltpu.VMEM(shape, F32)
    each = lambda *shape: [vm(*shape) for _ in range(2 * pieces)]
    copies = 2 * pieces * 26
    scratch = (
        [vm(n_c, n_y, n_zh, 8, hw + (META if k == 0 else 0)) for k in range(2 * pieces)]
        + each(n_x, n_zl, SLOTS, wc)
        + each(n_x, n_zl, SLOTS, wc)
        + each(n_zl, SLOTS, wc)
        + each(2, n_zl, SLOTS, wc)
        + each(n_zl, SLOTS, wc)
        + each(3, SLOTS, wc)
        + each(n_c, 2 * SLOTS, hw)
        + each(n_y, n_zh, 8, hw)
        + each(3, n_zh, 8, hw)
        + each(n_zh, 8, hw)
        + each(8, hw)
        + each(2, 8, hw)
        + [
            vm(2 * ff, width), vm(ff, width), vm(2 * ff, width), vm(ff, width),
            vm(2 * SLOTS, lanes), vm(2 * SLOTS, lanes),
            vm(lanes // n_c, n_c * 2 * SLOTS), vm(lanes // n_c, n_c * 2 * SLOTS),
            fl(2 * ff, n_dp * SLOTS), fl(ff, n_dp * SLOTS),
            vm(ff, n_dp * SLOTS), vm(n_dp * SLOTS, ff), vm(2 * ff, n_dp * SLOTS), vm(n_dp * SLOTS, 2 * ff),
            pltpu.SemaphoreType.DMA((copies,)), pltpu.SemaphoreType.DMA((copies,)),
            pltpu.SemaphoreType.DMA((3 + 3 * pieces,)),
        ]
    )
    any_space = pl.BlockSpec(memory_space=pl.ANY)
    vmem = pl.BlockSpec(memory_space=pltpu.VMEM)
    like = lambda a: jax.ShapeDtypeStruct(a.shape, BF16)
    return pl.pallas_call(
        functools.partial(kernel, sizes, pieces),
        out_shape=(like(tokens), like(tokens), like(gate_weight), like(gate_weight), like(gate_weight)),
        in_specs=[vmem, vmem, vmem, any_space, any_space, any_space],
        out_specs=(vmem, vmem, any_space, any_space, any_space),
        scratch_shapes=scratch,
        compiler_params=pltpu.CompilerParams(
            collective_id=0, has_side_effects=True, vmem_limit_bytes=56 * 2**20
        ),
        name="experts",
    )(tokens, out_grad, meta, gate_weight, up_weight, down_weight)


def solution(mesh):
    rows, held = P(("dp", "expert"), None), P("expert", "dp", None)
    return jax.shard_map(
        functools.partial(shards, SIZES, PIECES),
        mesh=mesh,
        in_specs=(rows, rows, rows, rows, held, held, held),
        out_specs=(rows, rows, held, held, held),
        check_vma=False,
    )
```

```python
import functools

import jax
import jax.numpy as jnp
from jax import lax
from jax.experimental import pallas as pl
from jax.experimental.pallas import tpu as pltpu
from jax.sharding import PartitionSpec as P

SIZES = (4, 4, 4, 4, 2)
PIECES = 4
ORDER = (
    0, 1, 2, 3, 4, 5, 6, 7, 10, 11, 12, 13, 20, 14, 30, 21, 15, 22, 16, 31, 32, 23, 17, 24, 25, 40, 33, 26, 27, 41,
    34, 42, 35, 50, 43, 36, 51, 44, 37, 52, 45, 60, 53, 61, 46, 54, 47, 62, 55, 63, 71, 80, 81, 56, 64, 57, 65, 90,
    82, 91, 83, 66, 67, 72, 100, 101, 102, 103, 110, 104, 105, 106, 107, 92, 111, 84, 93, 85, 120, 130, 112, 121,
    94, 131, 86, 113, 140, 95, 87, 122, 141, 114, 132, 123, 96, 115, 133, 142, 97, 150, 151, 124, 116, 134, 143,
    125, 135, 117, 144, 152, 126, 136, 145, 153, 127, 137, 146, 154, 155, 147, 156, 157,
)
SLOTS = 16
META = 128
F32 = jnp.float32
BF16 = jnp.bfloat16
MESH = pl.DeviceIdType.MESH


def nt(left, right):
    return lax.dot_general(left, right, (((1,), (1,)), ((), ())), preferred_element_type=F32)


def iota(shape, dim):
    return lax.broadcasted_iota(jnp.int32, shape, dim)


def ones_where(mask):
    return jnp.where(mask, 1.0, 0.0).astype(F32)


class Comm:
    def __init__(self, send, recv):
        self.send, self.recv, self.count, self.sent = send, recv, 0, []

    def reserve(self, amount):
        at = self.count
        self.count += amount
        return at

    def start(self, src, dst, device, sem):
        copy = pltpu.make_async_remote_copy(
            src_ref=src, dst_ref=dst, send_sem=self.send.at[sem], recv_sem=self.recv.at[sem],
            device_id=device, device_id_type=MESH,
        )
        copy.start()
        self.sent.append(copy)

    def arrived(self, dst, device, sem):
        pltpu.make_async_remote_copy(
            src_ref=dst, dst_ref=dst, send_sem=self.send.at[sem], recv_sem=self.recv.at[sem],
            device_id=device, device_id_type=MESH,
        ).wait_recv()

    def drain(self):
        for copy in self.sent:
            copy.wait_send()


class RingGather:
    def __init__(self, comm, buf, index, size, device, turn):
        self.comm, self.buf, self.i, self.n, self.device = comm, buf, index, size, device
        self.d = 1 if turn % 2 == 0 else -1
        self.sem = comm.reserve(3) if size > 1 else 0

    def at(self, step):
        return lax.rem(self.i + step + self.n, self.n)

    def near(self):
        if self.n == 1:
            return
        for j, step in enumerate((self.d, -self.d)):
            self.comm.start(self.buf.at[self.i], self.buf.at[self.i], self.device(self.at(step)), self.sem + j)

    def far(self):
        if self.n == 1:
            return
        back, ahead = self.at(-self.d), self.at(self.d)
        self.comm.arrived(self.buf.at[back], self.device(back), self.sem)
        self.comm.start(self.buf.at[back], self.buf.at[back], self.device(ahead), self.sem + 2)

    def finish(self):
        if self.n == 1:
            return
        ahead = self.at(self.d)
        self.comm.arrived(self.buf.at[ahead], self.device(ahead), self.sem + 1)
        self.comm.arrived(self.buf.at[self.at(2)], self.device(self.at(-self.d)), self.sem + 2)


class Spread:
    def __init__(self, comm, buf, index, size, device):
        self.comm, self.buf, self.i, self.n, self.device = comm, buf, index, size, device
        self.sem = comm.reserve(size - 1)

    def send(self):
        for j in range(1, self.n):
            self.comm.start(
                self.buf.at[self.i], self.buf.at[self.i], self.device(lax.rem(self.i + j, self.n)), self.sem + j - 1
            )

    def finish(self):
        for j in range(1, self.n):
            source = lax.rem(self.i + self.n - j, self.n)
            self.comm.arrived(self.buf.at[source], self.device(source), self.sem + j - 1)


class Collect:
    def __init__(self, comm, buf, near_buf, index, size, device):
        self.comm, self.buf, self.near_buf, self.i, self.n, self.device = comm, buf, near_buf, index, size, device
        self.sem = comm.reserve(size - 1)

    def send(self):
        for j in range(1, self.n):
            target = lax.rem(self.i + j, self.n)
            self.comm.start(self.buf.at[target], self.near_buf.at[j - 1], self.device(target), self.sem + j - 1)

    def total(self):
        value = self.buf[self.i].astype(F32)
        for j in range(1, self.n):
            source = lax.rem(self.i + self.n - j, self.n)
            self.comm.arrived(self.near_buf.at[j - 1], self.device(source), self.sem + j - 1)
            value = value + self.near_buf[j - 1].astype(F32)
        return value


class RingReduce:
    def __init__(self, comm, buf, far_buf, near_buf, index, size, device, turn):
        self.comm, self.buf, self.far_buf, self.near_buf = comm, buf, far_buf, near_buf
        self.i, self.n, self.device = index, size, device
        self.d = 1 if turn % 2 == 0 else -1
        self.sem = comm.reserve(3) if size > 1 else 0

    def at(self, step):
        return lax.rem(self.i + step + self.n, self.n)

    def first(self):
        if self.n == 1:
            return
        ahead, back = self.at(self.d), self.at(-self.d)
        self.comm.start(self.buf.at[self.at(2)], self.far_buf, self.device(ahead), self.sem)
        self.comm.start(self.buf.at[back], self.near_buf.at[1], self.device(back), self.sem + 1)

    def second(self):
        if self.n == 1:
            return
        ahead, back = self.at(self.d), self.at(-self.d)
        self.comm.arrived(self.far_buf, self.device(back), self.sem)
        self.buf[ahead] = (self.buf[ahead].astype(F32) + self.far_buf[...].astype(F32)).astype(BF16)
        self.comm.start(self.buf.at[ahead], self.near_buf.at[0], self.device(ahead), self.sem + 2)

    def total(self):
        own = self.buf[self.i].astype(F32)
        if self.n == 1:
            return own
        ahead, back = self.at(self.d), self.at(-self.d)
        self.comm.arrived(self.near_buf.at[1], self.device(ahead), self.sem + 1)
        self.comm.arrived(self.near_buf.at[0], self.device(back), self.sem + 2)
        return own + self.near_buf[0].astype(F32) + self.near_buf[1].astype(F32)


def kernel(
    sizes, pieces, tokens, out_grad, meta, w_gate, w_up, w_down, mixed, in_grad, g_gate, g_up, g_down, *scratch
):
    n_zl, n_x, n_zh, n_y, n_c = sizes
    n_dp, n_ex = n_zl * n_x, n_zh * n_y * n_c
    lanes = n_ex * 8
    half = lanes // n_c
    ff, width = w_gate.shape[1], w_gate.shape[2]
    wc = width // pieces
    hw = wc // 2
    items = range(2 * pieces)
    it = iter(scratch)
    per_item = lambda: [next(it) for _ in items]
    got, slots, part, x_far, x_near, x_sum, z_near, pair, back, y_near, y_sum, h_near = (
        per_item() for _ in range(12)
    )
    wgu, wdn, ggu, gdn, pick_x, pick_g, back_o, back_i, acc_gu, acc_d, hid, hid_t, gu, gu_t, before, plain, weighted = (
        next(it) for _ in range(17)
    )
    send, recv, local = (next(it) for _ in range(3))

    dp, ex = lax.axis_index("dp"), lax.axis_index("expert")
    x, zl = lax.rem(dp, n_x), lax.div(dp, n_x)
    c, y, zh = lax.rem(ex, n_c), lax.rem(lax.div(ex, n_c), n_y), lax.div(ex, n_c * n_y)

    to_x = lambda v: {"dp": zl * n_x + v, "expert": ex}
    to_zl = lambda v: {"dp": v * n_x + x, "expert": ex}
    to_c = lambda v: {"dp": dp, "expert": (zh * n_y + y) * n_c + v}
    to_y = lambda v: {"dp": dp, "expert": (zh * n_y + v) * n_c + c}
    to_zh = lambda v: {"dp": dp, "expert": (v * n_y + y) * n_c + c}

    partners = []
    for index, size, to in ((zh, n_zh, to_zh), (y, n_y, to_y), (zl, n_zl, to_zl)):
        partners += [to(lax.rem(index + j, size)) for j in range(1, size)]
    if n_x > 1:
        partners += [to_x(lax.rem(x + 1, n_x)), to_x(lax.rem(x + n_x - 1, n_x))]
    if n_c > 1:
        partners.append(to_c(1 - c))
    barrier = pltpu.get_barrier_semaphore()
    for partner in partners:
        pl.semaphore_signal(barrier, inc=1, device_id=partner, device_id_type=MESH)

    loads = [
        pltpu.make_async_copy(w_gate.at[0], wgu.at[pl.ds(0, ff)], local.at[0]),
        pltpu.make_async_copy(w_up.at[0], wgu.at[pl.ds(ff, ff)], local.at[1]),
        pltpu.make_async_copy(w_down.at[0], wdn, local.at[2]),
    ]
    for load in loads:
        load.start()

    def piece(k):
        lo = k % pieces * wc
        return slice(lo, lo + wc)

    for k in items:
        source, lo = tokens if k < pieces else out_grad, k % pieces * wc
        own = jnp.concatenate(
            [source[:, lo : lo + hw].astype(F32), source[:, lo + hw : lo + wc].astype(F32)], axis=0
        ).astype(BF16)
        if k == 0:
            got[k][c, y, zh, :, :META] = meta[...]
            got[k][c, y, zh, :, META:] = own
        else:
            got[k][c, y, zh] = own
    same = (iota((lanes, lanes), 0) % 8 < 4) == (iota((lanes, lanes), 1) % 8 < 4)
    before[...] = ones_where((iota((lanes, lanes), 0) < iota((lanes, lanes), 1)) & same).astype(BF16)
    pl.semaphore_wait(barrier, len(partners))

    comm = Comm(send, recv)
    in_zh = [Spread(comm, got[k].at[c, y], zh, n_zh, to_zh) for k in items]
    in_y = [Spread(comm, got[k].at[c], y, n_y, to_y) for k in items]
    in_c = [comm.reserve(1) for k in items]
    in_zl = [Spread(comm, slots[k].at[x], zl, n_zl, to_zl) for k in items]
    in_x = [RingGather(comm, slots[k], x, n_x, to_x, k) for k in items]
    out_x = [RingReduce(comm, part[k], x_far[k], x_near[k], x, n_x, to_x, k) for k in items]
    out_zl = [Collect(comm, x_sum[k], z_near[k], zl, n_zl, to_zl) for k in items]
    out_c = [comm.reserve(1) for k in items]
    out_y = [Collect(comm, back[k], y_near[k], y, n_y, to_y) for k in items]
    out_zh = [Collect(comm, y_sum[k], h_near[k], zh, n_zh, to_zh) for k in items]

    def make_pickers():
        rows = got[0][:, :, :, :, :META].astype(F32).reshape(lanes, META).astype(BF16)
        eye = ones_where(iota((8, META), 0) == iota((8, META), 1)).astype(BF16)
        facts = nt(eye, rows)
        id0, id1, w0, w1 = (facts[j : j + 1] for j in range(4))
        slot = iota((2 * SLOTS, lanes), 0)
        fits = ones_where((slot < SLOTS) == (iota((2 * SLOTS, lanes), 1) % 8 < 4))
        slot_f = (slot % SLOTS).astype(F32)
        for j in range(n_c):
            expert = (ex if j == 0 else ex + 1 - 2 * c).astype(F32)
            m0, m1 = ones_where(id0 == expert), ones_where(id1 == expert)
            routed = m0 + m1
            rank = jnp.dot(
                jnp.broadcast_to(routed, (8, lanes)).astype(BF16), before[...], preferred_element_type=F32
            )[0:1]
            hit = fits * ones_where(slot_f == rank) * routed
            plain[2 * SLOTS * j : 2 * SLOTS * (j + 1)] = hit
            weighted[2 * SLOTS * j : 2 * SLOTS * (j + 1)] = hit * (m0 * w0 + m1 * w1)
        pick_x[...] = plain[: 2 * SLOTS].astype(BF16)
        pick_g[...] = weighted[: 2 * SLOTS].astype(BF16)

    def turn_pickers():
        for ref, held in ((back_i, plain), (back_o, weighted)):
            flat = jnp.transpose(held[...])
            ref[...] = (flat if n_c == 1 else jnp.where(c == 0, flat[:half], flat[half:])).astype(BF16)


    def in_y_send(k):
        in_zh[k].finish()
        in_y[k].send()

    def in_core(k):
        in_y[k].finish()
        if n_c > 1:
            comm.start(got[k].at[c], got[k].at[c], to_c(1 - c), in_c[k])

    def in_pick(k):
        if n_c > 1:
            comm.arrived(got[k].at[1 - c], to_c(1 - c), in_c[k])
        if k == 0:
            make_pickers()
        lo = META if k == 0 else 0
        rows = got[k][:, :, :, :, lo:].astype(F32).reshape(lanes, hw).astype(BF16)
        picker = pick_x if k < pieces else pick_g
        picked = jnp.dot(picker[...], rows, preferred_element_type=F32).astype(BF16)
        slots[k][x, zl, :, :hw] = picked[:SLOTS]
        slots[k][x, zl, :, hw:] = picked[SLOTS:]
        in_zl[k].send()
        if k == 0:
            turn_pickers()

    def in_x_near(k):
        in_zl[k].finish()
        in_x[k].near()

    def rows_of(k):
        return slots[k][...].reshape(n_dp * SLOTS, wc)

    def in_products(k):
        in_x[k].finish()
        if k == 0:
            for load in loads:
                load.wait()
        weights, total = (wgu, acc_gu) if k < pieces else (wdn, acc_d)
        product = nt(weights[:, piece(k)], rows_of(k))
        total[...] = product if k % pieces == 0 else total[...] + product


    def activate(k):
        if k == 1:
            gate, up = acc_gu[:ff], acc_gu[ff:]
            sig = jax.nn.sigmoid(gate)
            silu = gate * sig
            hidden = silu * up
            hid[...] = hidden.astype(BF16)
            hid_t[...] = jnp.transpose(hidden).astype(BF16)
            acc_gu[:ff] = up * (sig * (1.0 + gate * (1.0 - sig)))
            acc_gu[ff:] = silu
        else:
            grad = acc_d[...]
            both = jnp.concatenate([grad * acc_gu[:ff], grad * acc_gu[ff:]], axis=0)
            gu[...] = both.astype(BF16)
            gu_t[...] = jnp.transpose(both).astype(BF16)


    def out_products(k):
        left, weights = (hid_t, wdn) if k < pieces else (gu_t, wgu)
        product = jnp.dot(left[...], weights[:, piece(k)], preferred_element_type=F32)
        part[k][...] = product.astype(BF16).reshape(n_x, n_zl, SLOTS, wc)
        out_x[k].first()

    stores = []

    def weight_grads(k):
        left, held = (gu, ggu) if k < pieces else (hid, gdn)
        held[:, piece(k)] = jnp.dot(left[...], rows_of(k), preferred_element_type=F32).astype(BF16)
        pairs = ((ggu, 0, g_gate), (ggu, ff, g_up)) if k < pieces else ((gdn, 0, g_down),)
        for ref, at, target in pairs:
            store = pltpu.make_async_copy(
                ref.at[pl.ds(at, ff), piece(k)], target.at[0, :, piece(k)], local.at[3 + len(stores)]
            )
            store.start()
            stores.append(store)

    def out_lines(k):
        x_sum[k][...] = out_x[k].total().astype(BF16)
        out_zl[k].send()

    def out_core(k):
        total = out_zl[k].total().astype(BF16)
        pair[k][0, :SLOTS] = total[:, :hw]
        pair[k][0, SLOTS:] = total[:, hw:]
        if n_c > 1:
            comm.start(pair[k].at[0], pair[k].at[1], to_c(1 - c), out_c[k])

    def out_back(k):
        if n_c > 1:
            comm.arrived(pair[k].at[1], to_c(1 - c), out_c[k])
        rows = pair[k][...].reshape(n_c * 2 * SLOTS, hw)
        spread = jnp.dot((back_o if k < pieces else back_i)[...], rows, preferred_element_type=F32)
        back[k][...] = spread.reshape(n_y, n_zh, 8, hw).astype(BF16)
        out_y[k].send()

    def out_zh_send(k):
        y_sum[k][...] = out_y[k].total().astype(BF16)
        out_zh[k].send()

    def out_store(k):
        total = out_zh[k].total()
        target, lo = mixed if k < pieces else in_grad, k % pieces * wc
        target[:, lo : lo + hw] = total[:4].astype(BF16)
        target[:, lo + hw : lo + wc] = total[4:].astype(BF16)

    steps = (
        lambda k: in_zh[k].send(),
        in_y_send,
        in_core,
        in_pick,
        in_x_near,
        lambda k: in_x[k].far(),
        in_products,
        activate,
        out_products,
        lambda k: out_x[k].second(),
        weight_grads,
        out_lines,
        out_core,
        out_back,
        out_zh_send,
        out_store,
    )
    for entry in ORDER:
        steps[entry // 10](entry % 10)
    comm.drain()
    for store in stores:
        store.wait()


def hand_out(*refs):
    copies = [pltpu.make_async_copy(refs[j], refs[5 + j], refs[10].at[j]) for j in range(5)]
    for copy in copies:
        copy.start()
    for copy in copies:
        copy.wait()


def shards(sizes, pieces, tokens, expert_ids, route_weights, out_grad, gate_weight, up_weight, down_weight):
    n_zl, n_x, n_zh, n_y, n_c = sizes
    n_dp, n_ex = n_zl * n_x, n_zh * n_y * n_c
    _, ff, width = gate_weight.shape
    wc = width // pieces
    hw = wc // 2
    lanes = n_ex * 8
    facts = jnp.concatenate([expert_ids.astype(BF16), route_weights], axis=1)
    meta = jnp.pad(jnp.concatenate([facts, facts], axis=0), ((0, 0), (0, META - 4)))
    vm = lambda *shape: pltpu.VMEM(shape, BF16)
    fl = lambda *shape: pltpu.VMEM(shape, F32)
    each = lambda *shape: [vm(*shape) for _ in range(2 * pieces)]
    copies = 2 * pieces * 26
    scratch = (
        [vm(n_c, n_y, n_zh, 8, hw + (META if k == 0 else 0)) for k in range(2 * pieces)]
        + each(n_x, n_zl, SLOTS, wc)
        + each(n_x, n_zl, SLOTS, wc)
        + each(n_zl, SLOTS, wc)
        + each(2, n_zl, SLOTS, wc)
        + each(n_zl, SLOTS, wc)
        + each(3, SLOTS, wc)
        + each(n_c, 2 * SLOTS, hw)
        + each(n_y, n_zh, 8, hw)
        + each(3, n_zh, 8, hw)
        + each(n_zh, 8, hw)
        + each(3, 8, hw)
        + [
            vm(2 * ff, width), vm(ff, width), vm(2 * ff, width), vm(ff, width),
            vm(2 * SLOTS, lanes), vm(2 * SLOTS, lanes),
            vm(lanes // n_c, n_c * 2 * SLOTS), vm(lanes // n_c, n_c * 2 * SLOTS),
            fl(2 * ff, n_dp * SLOTS), fl(ff, n_dp * SLOTS),
            vm(ff, n_dp * SLOTS), vm(n_dp * SLOTS, ff), vm(2 * ff, n_dp * SLOTS), vm(n_dp * SLOTS, 2 * ff),
            vm(lanes, lanes), fl(n_c * 2 * SLOTS, lanes), fl(n_c * 2 * SLOTS, lanes),
            pltpu.SemaphoreType.DMA((copies,)), pltpu.SemaphoreType.DMA((copies,)),
            pltpu.SemaphoreType.DMA((3 + 3 * pieces,)),
        ]
    )
    any_space = pl.BlockSpec(memory_space=pl.ANY)
    vmem = pl.BlockSpec(memory_space=pltpu.VMEM)
    hbm = pl.BlockSpec(memory_space=pltpu.HBM)
    like = lambda a: jax.ShapeDtypeStruct(a.shape, BF16)
    held = pl.pallas_call(
        functools.partial(kernel, sizes, pieces),
        out_shape=(like(tokens), like(tokens), like(gate_weight), like(gate_weight), like(gate_weight)),
        in_specs=[vmem, vmem, vmem, hbm, hbm, hbm],
        out_specs=(vmem, vmem, any_space, any_space, any_space),
        scratch_shapes=scratch,
        compiler_params=pltpu.CompilerParams(
            collective_id=0, has_side_effects=True, vmem_limit_bytes=51 * 2**20
        ),
        name="experts",
    )(tokens, out_grad, meta, gate_weight, up_weight, down_weight)
    return pl.pallas_call(
        hand_out,
        out_shape=tuple(like(a) for a in held),
        in_specs=[vmem] * 5,
        out_specs=[hbm] * 5,
        scratch_shapes=[pltpu.SemaphoreType.DMA((5,))],
        compiler_params=pltpu.CompilerParams(vmem_limit_bytes=8 * 2**20),
        name="results",
    )(*held)


def solution(mesh):
    rows, held = P(("dp", "expert"), None), P("expert", "dp", None)
    return jax.shard_map(
        functools.partial(shards, SIZES, PIECES),
        mesh=mesh,
        in_specs=(rows, rows, rows, rows, held, held, held),
        out_specs=(rows, rows, held, held, held),
        check_vma=False,
    )
```

```python
import functools

import jax
import jax.numpy as jnp
from jax import lax
from jax.experimental import pallas as pl
from jax.experimental.pallas import tpu as pltpu
from jax.sharding import PartitionSpec as P

SIZES = (4, 4, 4, 4, 2)
PIECES = 4
ORDER = (
    0, 1, 2, 3, 4, 5, 6, 7, 10, 11, 12, 13, 20, 14, 30, 21, 15, 22, 16, 31, 32, 23, 17, 24, 25, 40, 33, 26, 27, 41,
    34, 42, 35, 50, 43, 36, 51, 44, 37, 52, 45, 60, 53, 61, 46, 54, 47, 62, 55, 63, 71, 80, 81, 56, 64, 57, 65, 90,
    82, 91, 83, 66, 67, 72, 100, 101, 102, 103, 110, 104, 105, 106, 107, 92, 111, 84, 93, 85, 120, 130, 112, 121,
    94, 131, 86, 113, 140, 95, 87, 122, 141, 114, 132, 123, 96, 115, 133, 142, 97, 150, 151, 124, 116, 134, 143,
    125, 135, 117, 144, 152, 126, 136, 145, 153, 127, 137, 146, 154, 155, 147, 156, 157,
)
SLOTS = 16
META = 128
F32 = jnp.float32
BF16 = jnp.bfloat16
MESH = pl.DeviceIdType.MESH


def nt(left, right):
    return lax.dot_general(left, right, (((1,), (1,)), ((), ())), preferred_element_type=F32)


def iota(shape, dim):
    return lax.broadcasted_iota(jnp.int32, shape, dim)


def ones_where(mask):
    return jnp.where(mask, 1.0, 0.0).astype(F32)


class Comm:
    def __init__(self, send, recv):
        self.send, self.recv, self.count, self.sent = send, recv, 0, []

    def reserve(self, amount):
        at = self.count
        self.count += amount
        return at

    def start(self, src, dst, device, sem):
        copy = pltpu.make_async_remote_copy(
            src_ref=src, dst_ref=dst, send_sem=self.send.at[sem], recv_sem=self.recv.at[sem],
            device_id=device, device_id_type=MESH,
        )
        copy.start()
        self.sent.append(copy)

    def arrived(self, dst, device, sem):
        pltpu.make_async_remote_copy(
            src_ref=dst, dst_ref=dst, send_sem=self.send.at[sem], recv_sem=self.recv.at[sem],
            device_id=device, device_id_type=MESH,
        ).wait_recv()

    def drain(self):
        for copy in self.sent:
            copy.wait_send()


class RingGather:
    def __init__(self, comm, buf, index, size, device, turn):
        self.comm, self.buf, self.i, self.n, self.device = comm, buf, index, size, device
        self.d = 1 if turn % 2 == 0 else -1
        self.sem = comm.reserve(3) if size > 1 else 0

    def at(self, step):
        return lax.rem(self.i + step + self.n, self.n)

    def near(self):
        if self.n == 1:
            return
        for j, step in enumerate((self.d, -self.d)):
            self.comm.start(self.buf.at[self.i], self.buf.at[self.i], self.device(self.at(step)), self.sem + j)

    def far(self):
        if self.n == 1:
            return
        back, ahead = self.at(-self.d), self.at(self.d)
        self.comm.arrived(self.buf.at[back], self.device(back), self.sem)
        self.comm.start(self.buf.at[back], self.buf.at[back], self.device(ahead), self.sem + 2)

    def finish(self):
        if self.n == 1:
            return
        ahead = self.at(self.d)
        self.comm.arrived(self.buf.at[ahead], self.device(ahead), self.sem + 1)
        self.comm.arrived(self.buf.at[self.at(2)], self.device(self.at(-self.d)), self.sem + 2)


class LineRing:
    def __init__(self, comm, buf, index, size, line, lines, device, turn):
        self.comm, self.buf, self.i, self.n, self.device = comm, buf, index, size, device
        self.line, self.lines = line, lines
        self.d = 1 if turn % 2 == 0 else -1
        self.sem = comm.reserve(2 * lines + 1)

    def at(self, step):
        return lax.rem(self.i + step + self.n, self.n)

    def near(self, ahead):
        if self.n == 1:
            return
        block = self.buf.at[self.i, lax.rem(self.line + ahead, self.lines)]
        for j, step in enumerate((self.d, -self.d)):
            self.comm.start(block, block, self.device(self.at(step)), self.sem + 2 * ahead + j)

    def landed(self, step, j):
        source = self.at(step)
        for ahead in range(self.lines):
            block = self.buf.at[source, lax.rem(self.line + ahead, self.lines)]
            self.comm.arrived(block, self.device(source), self.sem + 2 * ahead + j)

    def far(self):
        if self.n == 1:
            return
        self.landed(-self.d, 0)
        back = self.buf.at[self.at(-self.d)]
        self.comm.start(back, back, self.device(self.at(self.d)), self.sem + 2 * self.lines)

    def finish(self):
        if self.n == 1:
            return
        self.landed(self.d, 1)
        self.comm.arrived(self.buf.at[self.at(2)], self.device(self.at(-self.d)), self.sem + 2 * self.lines)


class Spread:
    def __init__(self, comm, buf, index, size, device):
        self.comm, self.buf, self.i, self.n, self.device = comm, buf, index, size, device
        self.sem = comm.reserve(size - 1)

    def send(self):
        for j in range(1, self.n):
            self.comm.start(
                self.buf.at[self.i], self.buf.at[self.i], self.device(lax.rem(self.i + j, self.n)), self.sem + j - 1
            )

    def finish(self):
        for j in range(1, self.n):
            source = lax.rem(self.i + self.n - j, self.n)
            self.comm.arrived(self.buf.at[source], self.device(source), self.sem + j - 1)


class Collect:
    def __init__(self, comm, buf, near_buf, index, size, device):
        self.comm, self.buf, self.near_buf, self.i, self.n, self.device = comm, buf, near_buf, index, size, device
        self.sem = comm.reserve(size - 1)

    def send(self):
        for j in range(1, self.n):
            target = lax.rem(self.i + j, self.n)
            self.comm.start(self.buf.at[target], self.near_buf.at[j - 1], self.device(target), self.sem + j - 1)

    def total(self):
        value = self.buf[self.i].astype(F32)
        for j in range(1, self.n):
            source = lax.rem(self.i + self.n - j, self.n)
            self.comm.arrived(self.near_buf.at[j - 1], self.device(source), self.sem + j - 1)
            value = value + self.near_buf[j - 1].astype(F32)
        return value


class RingReduce:
    def __init__(self, comm, buf, far_buf, near_buf, index, size, device, turn):
        self.comm, self.buf, self.far_buf, self.near_buf = comm, buf, far_buf, near_buf
        self.i, self.n, self.device = index, size, device
        self.d = 1 if turn % 2 == 0 else -1
        self.sem = comm.reserve(3) if size > 1 else 0

    def at(self, step):
        return lax.rem(self.i + step + self.n, self.n)

    def first(self):
        if self.n == 1:
            return
        ahead, back = self.at(self.d), self.at(-self.d)
        self.comm.start(self.buf.at[self.at(2)], self.far_buf, self.device(ahead), self.sem)
        self.comm.start(self.buf.at[back], self.near_buf.at[1], self.device(back), self.sem + 1)

    def second(self):
        if self.n == 1:
            return
        ahead, back = self.at(self.d), self.at(-self.d)
        self.comm.arrived(self.far_buf, self.device(back), self.sem)
        self.buf[ahead] = (self.buf[ahead].astype(F32) + self.far_buf[...].astype(F32)).astype(BF16)
        self.comm.start(self.buf.at[ahead], self.near_buf.at[0], self.device(ahead), self.sem + 2)

    def total(self):
        own = self.buf[self.i].astype(F32)
        if self.n == 1:
            return own
        ahead, back = self.at(self.d), self.at(-self.d)
        self.comm.arrived(self.near_buf.at[1], self.device(ahead), self.sem + 1)
        self.comm.arrived(self.near_buf.at[0], self.device(back), self.sem + 2)
        return own + self.near_buf[0].astype(F32) + self.near_buf[1].astype(F32)


def kernel(
    sizes, pieces, tokens, out_grad, meta, w_gate, w_up, w_down, mixed, in_grad, g_gate, g_up, g_down, *scratch
):
    n_zl, n_x, n_zh, n_y, n_c = sizes
    n_dp, n_ex = n_zl * n_x, n_zh * n_y * n_c
    lanes = n_ex * 8
    half = lanes // n_c
    ff, width = w_gate.shape[1], w_gate.shape[2]
    wc = width // pieces
    hw = wc // 2
    items = range(2 * pieces)
    it = iter(scratch)
    per_item = lambda: [next(it) for _ in items]
    got, slots, part, x_far, x_near, x_sum, z_near, pair, back, y_near, y_sum, h_near = (
        per_item() for _ in range(12)
    )
    wgu, wdn, ggu, gdn, pick_x, pick_g, back_o, back_i, acc_gu, acc_d, hid, hid_t, gu, gu_t, before, plain, weighted = (
        next(it) for _ in range(17)
    )
    send, recv, local = (next(it) for _ in range(3))

    dp, ex = lax.axis_index("dp"), lax.axis_index("expert")
    x, zl = lax.rem(dp, n_x), lax.div(dp, n_x)
    c, y, zh = lax.rem(ex, n_c), lax.rem(lax.div(ex, n_c), n_y), lax.div(ex, n_c * n_y)

    to_x = lambda v: {"dp": zl * n_x + v, "expert": ex}
    to_zl = lambda v: {"dp": v * n_x + x, "expert": ex}
    to_c = lambda v: {"dp": dp, "expert": (zh * n_y + y) * n_c + v}
    to_y = lambda v: {"dp": dp, "expert": (zh * n_y + v) * n_c + c}
    to_zh = lambda v: {"dp": dp, "expert": (v * n_y + y) * n_c + c}

    partners = []
    for index, size, to in ((zh, n_zh, to_zh), (y, n_y, to_y), (zl, n_zl, to_zl)):
        partners += [to(lax.rem(index + j, size)) for j in range(1, size)]
    if n_x > 1:
        partners += [to_x(lax.rem(x + 1, n_x)), to_x(lax.rem(x + n_x - 1, n_x))]
    if n_c > 1:
        partners.append(to_c(1 - c))
    barrier = pltpu.get_barrier_semaphore()
    for partner in partners:
        pl.semaphore_signal(barrier, inc=1, device_id=partner, device_id_type=MESH)

    loads = [
        pltpu.make_async_copy(w_gate.at[0], wgu.at[pl.ds(0, ff)], local.at[0]),
        pltpu.make_async_copy(w_up.at[0], wgu.at[pl.ds(ff, ff)], local.at[1]),
        pltpu.make_async_copy(w_down.at[0], wdn, local.at[2]),
    ]
    for load in loads:
        load.start()

    def piece(k):
        lo = k % pieces * wc
        return slice(lo, lo + wc)

    of_token = ones_where(iota((8, META), 0) % 4 == iota((8, META), 1)).astype(BF16)
    for k in items:
        source, lo = tokens if k < pieces else out_grad, k % pieces * wc
        own = jnp.concatenate(
            [source[:, lo : lo + hw].astype(F32), source[:, lo + hw : lo + wc].astype(F32)], axis=0
        ).astype(BF16)
        if k == 0:
            got[k][c, y, zh, :, :META] = nt(of_token, meta[...]).astype(BF16)
            got[k][c, y, zh, :, META:] = own
        else:
            got[k][c, y, zh] = own
    same = (iota((lanes, lanes), 0) % 8 < 4) == (iota((lanes, lanes), 1) % 8 < 4)
    before[...] = ones_where((iota((lanes, lanes), 0) < iota((lanes, lanes), 1)) & same).astype(BF16)
    pl.semaphore_wait(barrier, len(partners))

    comm = Comm(send, recv)
    in_zh = [Spread(comm, got[k].at[c, y], zh, n_zh, to_zh) for k in items]
    in_y = [Spread(comm, got[k].at[c], y, n_y, to_y) for k in items]
    in_c = [comm.reserve(1) for k in items]
    in_zl = [Spread(comm, slots[k].at[x], zl, n_zl, to_zl) for k in items]
    in_x = [LineRing(comm, slots[k], x, n_x, zl, n_zl, to_x, k) for k in items]
    out_x = [RingReduce(comm, part[k], x_far[k], x_near[k], x, n_x, to_x, k) for k in items]
    out_zl = [Collect(comm, x_sum[k], z_near[k], zl, n_zl, to_zl) for k in items]
    out_c = [comm.reserve(1) for k in items]
    out_y = [Collect(comm, back[k], y_near[k], y, n_y, to_y) for k in items]
    out_zh = [Collect(comm, y_sum[k], h_near[k], zh, n_zh, to_zh) for k in items]

    def make_pickers():
        rows = got[0][:, :, :, :, :META].astype(F32).reshape(lanes, META).astype(BF16)
        eye = ones_where(iota((8, META), 0) == iota((8, META), 1)).astype(BF16)
        facts = nt(eye, rows)
        id0, id1, w0, w1 = (facts[j : j + 1] for j in range(4))
        slot = iota((2 * SLOTS, lanes), 0)
        fits = ones_where((slot < SLOTS) == (iota((2 * SLOTS, lanes), 1) % 8 < 4))
        slot_f = (slot % SLOTS).astype(F32)
        for j in range(n_c):
            expert = (ex if j == 0 else ex + 1 - 2 * c).astype(F32)
            m0, m1 = ones_where(id0 == expert), ones_where(id1 == expert)
            routed = m0 + m1
            rank = jnp.dot(
                jnp.broadcast_to(routed, (8, lanes)).astype(BF16), before[...], preferred_element_type=F32
            )[0:1]
            hit = fits * ones_where(slot_f == rank) * routed
            plain[2 * SLOTS * j : 2 * SLOTS * (j + 1)] = hit
            weighted[2 * SLOTS * j : 2 * SLOTS * (j + 1)] = hit * (m0 * w0 + m1 * w1)
        pick_x[...] = plain[: 2 * SLOTS].astype(BF16)
        pick_g[...] = weighted[: 2 * SLOTS].astype(BF16)

    def turn_pickers():
        for ref, held in ((back_i, plain), (back_o, weighted)):
            flat = jnp.transpose(held[...])
            ref[...] = (flat if n_c == 1 else jnp.where(c == 0, flat[:half], flat[half:])).astype(BF16)


    def in_y_send(k):
        in_zh[k].finish()
        in_y[k].send()

    def in_core(k):
        in_y[k].finish()
        if n_c > 1:
            comm.start(got[k].at[c], got[k].at[c], to_c(1 - c), in_c[k])

    def in_pick(k):
        if n_c > 1:
            comm.arrived(got[k].at[1 - c], to_c(1 - c), in_c[k])
        if k == 0:
            make_pickers()
        lo = META if k == 0 else 0
        rows = got[k][:, :, :, :, lo:].astype(F32).reshape(lanes, hw).astype(BF16)
        picker = pick_x if k < pieces else pick_g
        picked = jnp.dot(picker[...], rows, preferred_element_type=F32).astype(BF16)
        slots[k][x, zl, :, :hw] = picked[:SLOTS]
        slots[k][x, zl, :, hw:] = picked[SLOTS:]
        in_zl[k].send()
        in_x[k].near(0)
        if k == 0:
            turn_pickers()

    def in_x_near(k):
        in_zl[k].finish()
        for ahead in range(1, n_zl):
            in_x[k].near(ahead)

    def rows_of(k):
        return slots[k][...].reshape(n_dp * SLOTS, wc)

    def in_products(k):
        in_x[k].finish()
        if k == 0:
            for load in loads:
                load.wait()
        weights, total = (wgu, acc_gu) if k < pieces else (wdn, acc_d)
        product = nt(weights[:, piece(k)], rows_of(k))
        total[...] = product if k % pieces == 0 else total[...] + product


    def activate(k):
        if k == 1:
            gate, up = acc_gu[:ff], acc_gu[ff:]
            sig = jax.nn.sigmoid(gate)
            silu = gate * sig
            hidden = silu * up
            hid[...] = hidden.astype(BF16)
            hid_t[...] = jnp.transpose(hidden).astype(BF16)
            acc_gu[:ff] = up * (sig * (1.0 + gate * (1.0 - sig)))
            acc_gu[ff:] = silu
        else:
            grad = acc_d[...]
            both = jnp.concatenate([grad * acc_gu[:ff], grad * acc_gu[ff:]], axis=0)
            gu[...] = both.astype(BF16)
            gu_t[...] = jnp.transpose(both).astype(BF16)


    def out_products(k):
        left, weights = (hid_t, wdn) if k < pieces else (gu_t, wgu)
        product = jnp.dot(left[...], weights[:, piece(k)], preferred_element_type=F32)
        part[k][...] = product.astype(BF16).reshape(n_x, n_zl, SLOTS, wc)
        out_x[k].first()

    stores = []

    def weight_grads(k):
        left, held = (gu, ggu) if k < pieces else (hid, gdn)
        held[:, piece(k)] = jnp.dot(left[...], rows_of(k), preferred_element_type=F32).astype(BF16)
        pairs = ((ggu, 0, g_gate), (ggu, ff, g_up)) if k < pieces else ((gdn, 0, g_down),)
        for ref, at, target in pairs:
            store = pltpu.make_async_copy(
                ref.at[pl.ds(at, ff), piece(k)], target.at[0, :, piece(k)], local.at[3 + len(stores)]
            )
            store.start()
            stores.append(store)

    def out_lines(k):
        x_sum[k][...] = out_x[k].total().astype(BF16)
        out_zl[k].send()

    def out_core(k):
        total = out_zl[k].total().astype(BF16)
        pair[k][0, :SLOTS] = total[:, :hw]
        pair[k][0, SLOTS:] = total[:, hw:]
        if n_c > 1:
            comm.start(pair[k].at[0], pair[k].at[1], to_c(1 - c), out_c[k])

    def out_back(k):
        if n_c > 1:
            comm.arrived(pair[k].at[1], to_c(1 - c), out_c[k])
        rows = pair[k][...].reshape(n_c * 2 * SLOTS, hw)
        spread = jnp.dot((back_o if k < pieces else back_i)[...], rows, preferred_element_type=F32)
        back[k][...] = spread.reshape(n_y, n_zh, 8, hw).astype(BF16)
        out_y[k].send()

    def out_zh_send(k):
        y_sum[k][...] = out_y[k].total().astype(BF16)
        out_zh[k].send()

    def out_store(k):
        total = out_zh[k].total()
        target, lo = mixed if k < pieces else in_grad, k % pieces * wc
        target[:, lo : lo + hw] = total[:4].astype(BF16)
        target[:, lo + hw : lo + wc] = total[4:].astype(BF16)

    steps = (
        lambda k: in_zh[k].send(),
        in_y_send,
        in_core,
        in_pick,
        in_x_near,
        lambda k: in_x[k].far(),
        in_products,
        activate,
        out_products,
        lambda k: out_x[k].second(),
        weight_grads,
        out_lines,
        out_core,
        out_back,
        out_zh_send,
        out_store,
    )
    for entry in ORDER:
        steps[entry // 10](entry % 10)
    comm.drain()
    for store in stores:
        store.wait()


def hand_out(*refs):
    copies = [pltpu.make_async_copy(refs[j], refs[5 + j], refs[10].at[j]) for j in range(5)]
    for copy in copies:
        copy.start()
    for copy in copies:
        copy.wait()


def shards(sizes, pieces, tokens, expert_ids, route_weights, out_grad, gate_weight, up_weight, down_weight):
    n_zl, n_x, n_zh, n_y, n_c = sizes
    n_dp, n_ex = n_zl * n_x, n_zh * n_y * n_c
    _, ff, width = gate_weight.shape
    wc = width // pieces
    hw = wc // 2
    lanes = n_ex * 8
    facts = jnp.concatenate([expert_ids.T.astype(BF16), route_weights.T], axis=0)
    meta = jnp.pad(facts, ((0, META - 4), (0, META - 4)))
    vm = lambda *shape: pltpu.VMEM(shape, BF16)
    fl = lambda *shape: pltpu.VMEM(shape, F32)
    each = lambda *shape: [vm(*shape) for _ in range(2 * pieces)]
    copies = 2 * pieces * (24 + 2 * n_zl)
    scratch = (
        [vm(n_c, n_y, n_zh, 8, hw + (META if k == 0 else 0)) for k in range(2 * pieces)]
        + each(n_x, n_zl, SLOTS, wc)
        + each(n_x, n_zl, SLOTS, wc)
        + each(n_zl, SLOTS, wc)
        + each(2, n_zl, SLOTS, wc)
        + each(n_zl, SLOTS, wc)
        + each(3, SLOTS, wc)
        + each(n_c, 2 * SLOTS, hw)
        + each(n_y, n_zh, 8, hw)
        + each(3, n_zh, 8, hw)
        + each(n_zh, 8, hw)
        + each(3, 8, hw)
        + [
            vm(2 * ff, width), vm(ff, width), vm(2 * ff, width), vm(ff, width),
            vm(2 * SLOTS, lanes), vm(2 * SLOTS, lanes),
            vm(lanes // n_c, n_c * 2 * SLOTS), vm(lanes // n_c, n_c * 2 * SLOTS),
            fl(2 * ff, n_dp * SLOTS), fl(ff, n_dp * SLOTS),
            vm(ff, n_dp * SLOTS), vm(n_dp * SLOTS, ff), vm(2 * ff, n_dp * SLOTS), vm(n_dp * SLOTS, 2 * ff),
            vm(lanes, lanes), fl(n_c * 2 * SLOTS, lanes), fl(n_c * 2 * SLOTS, lanes),
            pltpu.SemaphoreType.DMA((copies,)), pltpu.SemaphoreType.DMA((copies,)),
            pltpu.SemaphoreType.DMA((3 + 3 * pieces,)),
        ]
    )
    any_space = pl.BlockSpec(memory_space=pl.ANY)
    vmem = pl.BlockSpec(memory_space=pltpu.VMEM)
    hbm = pl.BlockSpec(memory_space=pltpu.HBM)
    like = lambda a: jax.ShapeDtypeStruct(a.shape, BF16)
    held = pl.pallas_call(
        functools.partial(kernel, sizes, pieces),
        out_shape=(like(tokens), like(tokens), like(gate_weight), like(gate_weight), like(gate_weight)),
        in_specs=[vmem, vmem, vmem, hbm, hbm, hbm],
        out_specs=(vmem, vmem, any_space, any_space, any_space),
        scratch_shapes=scratch,
        compiler_params=pltpu.CompilerParams(
            collective_id=0, has_side_effects=True, vmem_limit_bytes=51 * 2**20
        ),
        name="experts",
    )(tokens, out_grad, meta, gate_weight, up_weight, down_weight)
    return pl.pallas_call(
        hand_out,
        out_shape=tuple(like(a) for a in held),
        in_specs=[vmem] * 5,
        out_specs=[hbm] * 5,
        scratch_shapes=[pltpu.SemaphoreType.DMA((5,))],
        compiler_params=pltpu.CompilerParams(vmem_limit_bytes=8 * 2**20),
        name="results",
    )(*held)


def solution(mesh):
    rows, held = P(("dp", "expert"), None), P("expert", "dp", None)
    return jax.shard_map(
        functools.partial(shards, SIZES, PIECES),
        mesh=mesh,
        in_specs=(rows, rows, rows, rows, held, held, held),
        out_specs=(rows, rows, held, held, held),
        check_vma=False,
    )
```
